32 devices in a mesh: row: 8 (over z, x), col: 4 (over y, core).
Axes of the slice: x: 2, y: 2, z: 4, core: 2. Of those that a mesh axis runs over, the one named last changes fastest.
Arguments:
- level_cot: float32 [128, 256, 128], P('col', 'row'), may hold values from -6 to 6
- level_state: float32 [128, 256, 128], P('col', 'row'), may hold values from -6 to 6
- momentum_cot: float32 [3, 128, 256, 128], P(None, 'col', 'row'), may hold values from -6 to 6
- courant: float32 [128, 256, 128], P('col', 'row'), may hold values from 0.05 to 0.3
- stencil: int32 [128, 256, 128], P('col', 'row'), may hold values from 0 to 2
- upwind: int32 [128, 256, 128], P('col', 'row'), may hold values from 0 to 1
- viscosity: float32 [128, 256, 128], P('col', 'row'), may hold values from 0.3 to 3
- band_cells: int32 [4, 8, 4096], P('col', 'row'), may hold values from 1 to 131070, as said below
- band_count: int32 [4, 8], P('col', 'row'), may hold values from 1024 to 4096, as said below
- band_force: float32 [3, 4, 8, 4096], P(None, 'col', 'row'), may hold values from -6 to 6
- design_basis: float32 [16, 128, 256], P(None, 'col', 'row')
Outputs:
- level_adjoint: float32 [128, 256, 128], P('col', 'row')
- momentum_adjoint: float32 [3, 128, 256, 128], P(None, 'col', 'row')
- design_grad: float32 [8, 16], P('row')
The draws below stay inside these ranges and needn't reach their ends.
Inputs may be any that keep to these rules, and one draw needn't show every extreme that they name: `band_count`: every nozzle's live band entries are at least 1024, and some nozzle has exactly 4096. `band_cells`: each entry is (x 32 + y) * 128 + z for a cell (x, y, z) of the nozzle's block with z from 1 to 126; cells may repeat.
All inputs are finite; a program needn't handle non-finite values.
Results may differ from the reference program's by a relative error of at most 0.00002.
Values sent between devices are 32-bit elements; how exact they have to be, the bound alone decides.
A program may use at most 192 MiB of HBM per device.

```python
import math
import jax
import jax.numpy as jnp
from jax import lax

CX = 32
CY = 32
CZ = 128
BAND_CAP = 4096
NDES = 16
SUBSTEPS = 6
COLS = 4
ROWS = 8
NX = 128
NY = 256
NZ = 128
N_ROW = 8
N_COL = 4


def draw_band_count(key, part):
    first_key, second_key = jax.random.split(jax.random.fold_in(key, 11))
    counts = jax.random.randint(first_key, (COLS * ROWS,), BAND_CAP // 4, BAND_CAP + 1)
    chosen = jax.random.randint(second_key, (), 0, COLS * ROWS)
    counts = jnp.where(jnp.arange(COLS * ROWS) == chosen, BAND_CAP, counts)
    return counts.reshape(COLS, ROWS).astype(jnp.int32)


def draw_band_cells(key, part):
    key_x, key_y, key_z = jax.random.split(jax.random.fold_in(key, 23), 3)
    cells_x = jax.random.randint(key_x, (COLS, ROWS, BAND_CAP), 0, CX)
    cells_y = jax.random.randint(key_y, (COLS, ROWS, BAND_CAP), 0, CY)
    cells_z = jax.random.randint(key_z, (COLS, ROWS, BAND_CAP), 1, CZ - 1)
    return ((cells_x * CY + cells_y) * CZ + cells_z).astype(jnp.int32)


def draw_design_basis(key, part):
    inner = jax.random.fold_in(key, 37)
    position = jnp.arange(NX, dtype=jnp.float32) / NX
    base = jax.random.normal(inner, (NDES, NX, NY), jnp.float32)
    slope = 2.0
    scale = 1.0 + slope * position
    return (base * scale[None, :, None]).astype(jnp.float32)


def place_ends(values, rng, least, high):
    extent = values.shape
    index_at = [jax.random.randint(jax.random.fold_in(rng, axis), (), 0, extent[axis]) for axis in range(len(extent))]
    values = values.at[tuple(index_at)].set(least)
    longest = extent.index(max(extent))
    index_at[longest] = (index_at[longest] + 1) % extent[longest]
    return values.at[tuple(index_at)].set(high)


def levels(key, shape, cuts, least, high):
    def one(dim, shards_of):
        draws = jax.random.uniform(jax.random.fold_in(jax.random.fold_in(key, 6), dim), (shards_of,), jnp.float32, least / len(cuts), high / len(cuts))
        return jnp.repeat(jnp.exp(draws), shape[dim] // shards_of).reshape((-1,) + (1,) * (len(shape) - dim - 1))

    loudness = one(*cuts[0])
    for cut in cuts[1:]:
        loudness = loudness * one(*cut)
    return loudness


def scatter_about(key, dims, scale, limit, cuts=(), kind=jnp.bfloat16):
    drawn = scale * jax.random.normal(key, dims, jnp.float32)
    if cuts:
        drawn = drawn * levels(key, dims, cuts, -0.22, 0.18)
    return jnp.clip(drawn, -limit, limit).astype(kind)


def setup_inputs(seed: int = 0) -> dict:
    keys = jax.random.split(jax.random.key(seed), 12)
    level_cot = scatter_about(keys[0], (NX, NY, NZ), 1.0, 6.0, ((0, 4), (1, 8)), jnp.float32)
    level_state = scatter_about(keys[1], (NX, NY, NZ), 1.0, 6.0, ((0, 4), (1, 8)), jnp.float32)
    momentum_cot = scatter_about(keys[2], (3, NX, NY, NZ), 1.0, 6.0, ((1, 4), (2, 8)), jnp.float32)
    courant = jnp.clip(jnp.exp(math.log(0.3) - 1.7917595 * jax.random.uniform(keys[3], (NX, NY, NZ), jnp.float32) ** levels(keys[3], (NX, NY, NZ), ((0, 4), (1, 8)), -0.2, 0.2)), 0.05, 0.3)
    stencil = place_ends(jax.random.randint(keys[4], (NX, NY, NZ), 0, 3), jax.random.fold_in(keys[4], 1), 0, 2).astype(jnp.int32)
    upwind = place_ends(jax.random.randint(keys[5], (NX, NY, NZ), 0, 2), jax.random.fold_in(keys[5], 1), 0, 1).astype(jnp.int32)
    viscosity = jnp.clip(jnp.exp(math.log(3.0) - 2.3025851 * jax.random.uniform(keys[6], (NX, NY, NZ), jnp.float32) ** levels(keys[6], (NX, NY, NZ), ((0, 4), (1, 8)), -0.2, 0.2)), 0.3, 3.0)
    band_cells = draw_band_cells(jax.random.fold_in(keys[11], 71), 0)
    band_count = draw_band_count(jax.random.fold_in(keys[11], 71), 0)
    band_force = scatter_about(keys[9], (3, COLS, ROWS, BAND_CAP), 1.0, 6.0, ((1, 4), (2, 8)), jnp.float32)
    design_basis = draw_design_basis(jax.random.fold_in(keys[11], 71), 0)
    return dict(level_cot=level_cot, level_state=level_state, momentum_cot=momentum_cot, courant=courant, stencil=stencil, upwind=upwind, viscosity=viscosity, band_cells=band_cells, band_count=band_count, band_force=band_force, design_basis=design_basis)


candidate_weights = ((1.0 / 3.0, -7.0 / 6.0, 11.0 / 6.0, 0.0, 0.0, 0.0), (0.0, -1.0 / 6.0, 5.0 / 6.0, 1.0 / 3.0, 0.0, 0.0), (0.0, 0.0, 1.0 / 3.0, 5.0 / 6.0, -1.0 / 6.0, 0.0), (0.0, 0.0, 0.0, 11.0 / 6.0, -7.0 / 6.0, 1.0 / 3.0), (0.0, 0.0, 1.0 / 3.0, 5.0 / 6.0, -1.0 / 6.0, 0.0), (0.0, -1.0 / 6.0, 5.0 / 6.0, 1.0 / 3.0, 0.0, 0.0))
rate_value = 0.05

def offset_weights(face_code):
    result = []
    for offset in range(6):
        accum = jnp.zeros(face_code.shape, jnp.float32)
        for candidate in range(6):
            value = candidate_weights[candidate][offset]
            if value != 0.0:
                accum = accum + jnp.where(face_code == candidate, value, 0.0).astype(jnp.float32)
        result.append(accum)
    return result

def diffuse(padded_field, padded_mu):
    centre = padded_field[:, 1:-1, 1:-1]
    mu_centre = padded_mu[1:-1, 1:-1]
    accum = jnp.zeros_like(centre)
    pairs = ((padded_field[:, 2:, 1:-1], padded_mu[2:, 1:-1]), (padded_field[:, :-2, 1:-1], padded_mu[:-2, 1:-1]), (padded_field[:, 1:-1, 2:], padded_mu[1:-1, 2:]), (padded_field[:, 1:-1, :-2], padded_mu[1:-1, :-2]))
    for near_field, near_mu in pairs:
        accum = accum + 0.5 * (mu_centre + near_mu) * (near_field - centre)
    upper = jnp.pad(centre[..., 1:], ((0, 0), (0, 0), (0, 0), (0, 1)))
    lower = jnp.pad(centre[..., :-1], ((0, 0), (0, 0), (0, 0), (1, 0)))
    mu_upper = jnp.pad(mu_centre[..., 1:], ((0, 0), (0, 0), (0, 1)))
    mu_lower = jnp.pad(mu_centre[..., :-1], ((0, 0), (0, 0), (1, 0)))
    accum = accum + 0.5 * (mu_centre + mu_upper) * (upper - centre)
    accum = accum + 0.5 * (mu_centre + mu_lower) * (lower - centre)
    return accum

def reference(level_cot, level_state, momentum_cot, courant, stencil, upwind, viscosity, band_cells, band_count, band_force, design_basis):
    face_code = stencil + 3 * upwind
    weights = offset_weights(face_code)
    padded_state = jnp.pad(level_state, ((2, 3), (0, 0), (0, 0)))
    face_value = jnp.zeros_like(level_state)
    for offset in range(6):
        face_value = face_value + weights[offset] * padded_state[offset:offset + NX]
    inside = (jnp.arange(NX) < NX - 1)[:, None, None]
    face_speed = jnp.where(inside, courant * (1 - 2 * upwind).astype(jnp.float32), 0.0)
    ahead = jnp.pad(level_cot[1:], ((0, 1), (0, 0), (0, 0)))
    cot_jump = ahead - level_cot
    weighted = cot_jump * face_speed
    spread = jnp.zeros((NX + 5, NY, NZ), jnp.float32)
    for offset in range(6):
        spread = spread + jnp.pad(weighted * weights[offset], ((offset, 5 - offset), (0, 0), (0, 0)))
    level_base = level_cot + spread[2:2 + NX]
    local_x = band_cells // (CY * CZ)
    local_y = band_cells // CZ % CY
    local_z = band_cells % CZ
    global_x = local_x + (jnp.arange(N_COL, dtype=jnp.int32) * CX)[:, None, None]
    global_y = local_y + (jnp.arange(N_ROW, dtype=jnp.int32) * CY)[None, :, None]
    flat_index = ((global_x * NY + global_y) * NZ + local_z).reshape(-1).astype(jnp.int32)
    is_live = (jnp.arange(BAND_CAP, dtype=jnp.int32)[None, None, :] < band_count[:, :, None]).reshape(-1)
    picked = momentum_cot.reshape(3, -1)[:, flat_index]
    strength = jnp.where(is_live, lax.optimization_barrier(jnp.sum(band_force.reshape(3, -1) * picked, axis=0)), 0.0)
    level_flat = level_base.reshape(-1)
    level_flat = level_flat.at[flat_index].add(-2.0 * strength)
    level_flat = level_flat.at[flat_index + 1].add(strength)
    level_flat = level_flat.at[flat_index - 1].add(strength)
    level_adjoint = level_flat.reshape(NX, NY, NZ)
    padded_mu = jnp.pad(viscosity, ((1, 1), (1, 1), (0, 0)))
    momentum = momentum_cot
    for substep in range(SUBSTEPS):
        padded_field = jnp.pad(momentum, ((0, 0), (1, 1), (1, 1), (0, 0)))
        momentum = momentum + rate_value * diffuse(padded_field, padded_mu)
    sensitivity = lax.optimization_barrier(jnp.sum(cot_jump * face_value * face_speed, axis=2))
    partial_value = lax.optimization_barrier(jnp.sum(design_basis * sensitivity[None], axis=1))
    design_grad = lax.optimization_barrier(jnp.sum(partial_value.reshape(NDES, N_ROW, CY), axis=2)).T / math.sqrt(NX * CY * NZ)
    return (level_adjoint, momentum, design_grad)
```

```python
import functools
import math

import jax
import jax.numpy as jnp
from jax import lax
from jax.experimental import pallas as pl
from jax.experimental.pallas import tpu as pltpu
from jax.sharding import PartitionSpec as P

MESH = pl.DeviceIdType.MESH
RATE = 0.05
W1 = 4
W2 = 2
CHUNK = 512
FACES = 3


def kernel(
    n_row,
    n_col,
    cot_hbm,
    state_hbm,
    mom_hbm,
    courant_hbm,
    stencil_hbm,
    upwind_hbm,
    visc_hbm,
    cells_ref,
    count_ref,
    force_ref,
    basis_ref,
    level_out,
    mom_out,
    grad_out,
    field,
    other,
    coef,
    lev,
    codes,
    band_sum,
    product,
    pack_lo,
    pack_hi,
    got_lo,
    got_hi,
    pack2_lo,
    pack2_hi,
    got2_lo,
    got2_hi,
    side2_lo,
    side2_hi,
    mine,
    partials,
    local_sem,
    send_sem,
    recv_sem,
    part_send,
    part_recv,
):
    nx, ny, nz = cot_hbm.shape
    row = lax.axis_index("row")
    col = lax.axis_index("col")
    has = {
        ("row", -1): row > 0,
        ("row", 1): row < n_row - 1,
        ("col", -1): col > 0,
        ("col", 1): col < n_col - 1,
    }

    def exists(dr, dc):
        cond = None
        for axis, d in (("row", dr), ("col", dc)):
            if d:
                here = has[(axis, d)]
                cond = here if cond is None else jnp.logical_and(cond, here)
        return cond

    barrier = pltpu.get_barrier_semaphore()
    expected = jnp.int32(n_col - 1)
    for d in range(1, n_col):
        pl.semaphore_signal(
            barrier, inc=1, device_id=(row, lax.rem(col + d, n_col)), device_id_type=MESH
        )
    for dr in (-1, 1):
        for dc in (-1, 0, 1):
            cond = exists(dr, dc)

            @pl.when(cond)
            def _(dr=dr, dc=dc):
                pl.semaphore_signal(
                    barrier, inc=1, device_id=(row + dr, col + dc), device_id_type=MESH
                )

            expected = expected + jnp.where(cond, 1, 0).astype(jnp.int32)

    local = []

    def fetch(src, dst):
        copy = pltpu.make_async_copy(src, dst, local_sem.at[len(local)])
        copy.start()
        local.append(copy)

    for k in range(3):
        fetch(mom_hbm.at[k], field.at[k, W1 : W1 + nx, 0:ny])
    fetch(visc_hbm, field.at[3, W1 : W1 + nx, 0:ny])
    for slot, src in enumerate((cot_hbm, state_hbm, courant_hbm)):
        fetch(src, lev.at[slot, FACES : FACES + nx])
    for slot, src in enumerate((stencil_hbm, upwind_hbm)):
        fetch(src, codes.at[slot, FACES : FACES + nx])

    sends = []

    def remote(src, dst, dr, dc):
        i = len(sends)
        copy = pltpu.make_async_remote_copy(
            src_ref=src,
            dst_ref=dst,
            send_sem=send_sem.at[i],
            recv_sem=recv_sem.at[i],
            device_id=(row + dr, col + dc),
            device_id_type=MESH,
        )

        @pl.when(exists(dr, dc))
        def _():
            copy.start()

        sends.append((copy, dr, dc))
        return sends[-1]

    def arrived(entry):
        copy, dr, dc = entry

        @pl.when(exists(-dr, -dc))
        def _():
            copy.wait_recv()

    def departed(entry):
        copy, dr, dc = entry

        @pl.when(exists(dr, dc))
        def _():
            copy.wait_send()

    for copy in local[:4]:
        copy.wait()

    def pack(x, _):
        for k in range(4):
            pack_lo[k, x] = field[k, W1 + x, 0:8][0:W1]
            pack_hi[k, x] = field[k, W1 + x, ny - 8 : ny][8 - W1 : 8]
        return 0

    lax.fori_loop(0, nx, pack, 0)
    pl.semaphore_wait(barrier, expected)

    first = [
        remote(pack_hi, got_lo.at[:, W1 : W1 + nx], 1, 0),
        remote(pack_lo, got_hi.at[:, W1 : W1 + nx], -1, 0),
        remote(pack_hi.at[:, nx - W1 : nx], got_lo.at[:, 0:W1], 1, 1),
        remote(pack_hi.at[:, 0:W1], got_lo.at[:, W1 + nx : 2 * W1 + nx], 1, -1),
        remote(pack_lo.at[:, nx - W1 : nx], got_hi.at[:, 0:W1], -1, 1),
        remote(pack_lo.at[:, 0:W1], got_hi.at[:, W1 + nx : 2 * W1 + nx], -1, -1),
    ]
    for copy in local[4:]:
        copy.wait()
    level_sends = [
        remote(lev.at[:, nx : nx + FACES], lev.at[:, 0:FACES], 0, 1),
        remote(codes.at[:, nx : nx + FACES], codes.at[:, 0:FACES], 0, 1),
        remote(lev.at[:, FACES : 2 * FACES], lev.at[:, nx + FACES : nx + 2 * FACES], 0, -1),
        remote(codes.at[:, FACES : 2 * FACES], codes.at[:, nx + FACES : nx + 2 * FACES], 0, -1),
    ]
    first += [
        remote(field.at[:, nx : nx + W1, 0:ny], field.at[:, 0:W1, 0:ny], 0, 1),
        remote(
            field.at[:, W1 : 2 * W1, 0:ny], field.at[:, nx + W1 : nx + 2 * W1, 0:ny], 0, -1
        ),
    ]

    count = count_ref[0, 0]
    band_cap = cells_ref.shape[-1]

    def band(step, _):
        at = pl.multiple_of(step * CHUNK, CHUNK)
        cell = cells_ref[0, :, pl.ds(at, CHUNK)]
        entry = at + lax.broadcasted_iota(jnp.int32, (1, CHUNK), 1)
        line = cell // nz
        z = cell - line * nz
        lines = lax.broadcasted_iota(jnp.int32, (nx * ny, CHUNK), 0) == line
        left = jnp.where(lines, 1.0, 0.0).astype(jnp.bfloat16)
        hit = lax.broadcasted_iota(jnp.int32, (nz, CHUNK), 0) == z
        parts = []
        for k in range(3):
            force = jnp.where(entry < count, force_ref[k, 0, :, pl.ds(at, CHUNK)], 0.0)
            high = force.astype(jnp.bfloat16).astype(jnp.float32)
            for part in (high, force - high):
                parts.append(jnp.where(hit, part, 0.0).astype(jnp.bfloat16))
        right = jnp.concatenate(parts, axis=0)
        total = lax.dot_general(
            left, right, (((1,), (1,)), ((), ())), preferred_element_type=jnp.float32
        )

        @pl.when(step == 0)
        def _():
            band_sum[...] = total

        @pl.when(step > 0)
        def _():
            band_sum[...] += total

        return 0

    lax.fori_loop(0, band_cap // CHUNK, band, 0)

    for entry in level_sends:
        arrived(entry)

    @pl.when(jnp.logical_not(has[("col", -1)]))
    def _():
        lev[:, 0:FACES] = jnp.zeros((3, FACES, ny, nz), jnp.float32)
        codes[:, 0:FACES] = jnp.zeros((2, FACES, ny, nz), jnp.int32)

    @pl.when(jnp.logical_not(has[("col", 1)]))
    def _():
        lev[:, nx + FACES : nx + 2 * FACES] = jnp.zeros((3, FACES, ny, nz), jnp.float32)
        codes[:, nx + FACES : nx + 2 * FACES] = jnp.zeros((2, FACES, ny, nz), jnp.int32)

    def face(e, carry, with_product, with_out):
        up = codes[1, e]
        sten = codes[0, e]
        below = up == 0
        is_a = jnp.logical_and(below, sten == 0)
        is_d = jnp.logical_and(jnp.logical_not(below), sten == 0)
        is_b = sten == jnp.where(below, 1, 2)
        g = col * nx + e - FACES
        inside = jnp.logical_and(g >= 0, g < n_col * nx - 1)
        speed = lev[2, e] * jnp.where(below, 1.0, -1.0)
        speed = jnp.where(inside, speed, 0.0)
        weighted = (lev[0, e + 1] - lev[0, e]) * speed
        zero = 0.0
        wts = (
            jnp.where(is_a, 1 / 3, zero),
            jnp.where(is_a, -7 / 6, jnp.where(is_b, -1 / 6, zero)),
            jnp.where(is_a, 11 / 6, jnp.where(is_b, 5 / 6, jnp.where(is_d, zero, 1 / 3))),
            jnp.where(is_d, 11 / 6, jnp.where(is_b, 1 / 3, jnp.where(is_a, zero, 5 / 6))),
            jnp.where(is_d, -7 / 6, jnp.where(jnp.logical_or(is_a, is_b), zero, -1 / 6)),
            jnp.where(is_d, 1 / 3, zero),
        )
        sums = [c + weighted * w for c, w in zip(carry, wts)]
        if with_product:
            value = wts[0] * lev[1, e - 2]
            for m in range(1, 6):
                value = value + wts[m] * lev[1, e - 2 + m]
            at = pl.multiple_of((e - FACES) * ny, ny)
            product[pl.ds(at, ny), :] = weighted * value
        if with_out:
            j = e - 5
            at = pl.multiple_of(j * ny, ny)
            strength = jnp.zeros((ny, nz), jnp.float32)
            for k in range(3):
                force = (
                    band_sum[pl.ds(at, ny), 2 * k * nz : (2 * k + 1) * nz]
                    + band_sum[pl.ds(at, ny), (2 * k + 1) * nz : (2 * k + 2) * nz]
                )
                strength = strength + force * field[k, W1 + j, 0:ny]
            bend = pltpu.roll(strength, 1, 1) + pltpu.roll(strength, nz - 1, 1) - 2.0 * strength
            level_out[j] = lev[0, j + FACES] + sums[0] + bend
        return tuple(sums[1:]) + (jnp.zeros((ny, nz), jnp.float32),)

    carry = tuple(jnp.zeros((ny, nz), jnp.float32) for _ in range(6))
    for low, high, with_product, with_out in (
        (0, 3, False, False),
        (3, 5, True, False),
        (5, nx + 3, True, True),
        (nx + 3, nx + 5, False, True),
    ):
        carry = lax.fori_loop(
            low,
            high,
            functools.partial(face, with_product=with_product, with_out=with_out),
            carry,
        )
    mine[...] = jnp.dot(
        basis_ref[...],
        product[...],
        precision=lax.Precision.HIGHEST,
        preferred_element_type=jnp.float32,
    )
    part_copies = []
    for d in range(1, n_col):
        copy = pltpu.make_async_remote_copy(
            src_ref=mine,
            dst_ref=partials.at[d],
            send_sem=part_send.at[d],
            recv_sem=part_recv.at[d],
            device_id=(row, lax.rem(col + d, n_col)),
            device_id_type=MESH,
        )
        copy.start()
        part_copies.append(copy)

    for entry in first:
        arrived(entry)

    def line_of(x, width, lo_ref, hi_ref, k):
        left = x < width
        right = x >= width + nx
        in_col = jnp.logical_and(
            jnp.logical_or(jnp.logical_not(left), has[("col", -1)]),
            jnp.logical_or(jnp.logical_not(right), has[("col", 1)]),
        )
        hi = jnp.where(jnp.logical_and(in_col, has[("row", 1)]), hi_ref[k, x], 0.0)
        lo = jnp.where(jnp.logical_and(in_col, has[("row", -1)]), lo_ref[k, x], 0.0)
        return hi, lo

    def unpack(x, _):
        for k in range(4):
            hi, lo = line_of(x, W1, got_lo, got_hi, k)
            field[k, x, ny : ny + 8] = jnp.concatenate([hi, lo], axis=0)
        return 0

    lax.fori_loop(0, nx + 2 * W1, unpack, 0)

    @pl.when(jnp.logical_not(has[("col", -1)]))
    def _():
        field[:, 0:W1, 0:ny] = jnp.zeros((4, W1, ny, nz), jnp.float32)

    @pl.when(jnp.logical_not(has[("col", 1)]))
    def _():
        field[:, nx + W1 : nx + 2 * W1, 0:ny] = jnp.zeros((4, W1, ny, nz), jnp.float32)

    tall = ny + 8
    sub = lax.broadcasted_iota(jnp.int32, (tall, nz), 0)
    lane = lax.broadcasted_iota(jnp.int32, (tall, nz), 1)
    up_there = jnp.where(has[("row", 1)], 1, 0)
    down_there = jnp.where(has[("row", -1)], 1, 0)
    y_inside = jnp.where(sub < ny, 1, jnp.where(sub < ny + 4, up_there, down_there)) > 0

    def coefficients(x, _):
        left = jnp.where(x < W1, jnp.where(has[("col", -1)], 1, 0), 1)
        right = jnp.where(x >= W1 + nx, jnp.where(has[("col", 1)], 1, 0), 1)
        inside = jnp.logical_and(y_inside, left * right > 0)
        mu = field[3, x]
        half = 0.5 * RATE
        near = [
            half * (mu + field[3, x + 1]),
            half * (mu + field[3, x - 1]),
            half * (mu + pltpu.roll(mu, tall - 1, 0)),
            half * (mu + pltpu.roll(mu, 1, 0)),
            half * (mu + jnp.where(lane == nz - 1, 0.0, pltpu.roll(mu, nz - 1, 1))),
            half * (mu + jnp.where(lane == 0, 0.0, pltpu.roll(mu, 1, 1))),
        ]
        own = 1.0 - (((near[0] + near[1]) + (near[2] + near[3])) + (near[4] + near[5]))
        near[4] = jnp.where(lane == nz - 1, 0.0, near[4])
        near[5] = jnp.where(lane == 0, 0.0, near[5])
        for slot, value in enumerate([own] + near):
            coef[slot, x] = jnp.where(inside, value, 0.0)
        return 0

    lax.fori_loop(1, nx + 2 * W1 - 1, coefficients, 0)

    def advance(src, dst, low, high, last):
        def one(x, _):
            for k in range(3):
                v = src[k, x]
                new = (
                    coef[0, x] * v
                    + coef[1, x] * src[k, x + 1]
                    + coef[2, x] * src[k, x - 1]
                    + coef[3, x] * pltpu.roll(v, tall - 1, 0)
                    + coef[4, x] * pltpu.roll(v, 1, 0)
                    + coef[5, x] * pltpu.roll(v, nz - 1, 1)
                    + coef[6, x] * pltpu.roll(v, 1, 1)
                )
                if last:
                    dst[k, x - W1] = new[0:ny]
                else:
                    dst[k, x] = new
            return 0

        lax.fori_loop(low, high, one, 0)

    end = nx + 2 * W1
    advance(field, other, 1, end - 1, False)
    for entry in first[-2:]:
        departed(entry)
    advance(other, field, 2, end - 2, False)
    advance(field, other, 3, end - 3, False)
    advance(other, field, 4, end - 4, False)

    def pack2(x, _):
        for k in range(3):
            pack2_lo[k, x] = field[k, W1 + x, 0:8][0:W2]
            pack2_hi[k, x] = field[k, W1 + x, ny - 8 : ny][8 - W2 : 8]
        return 0

    lax.fori_loop(0, nx, pack2, 0)
    second = [
        remote(pack2_hi, got2_lo.at[:, W2 : W2 + nx], 1, 0),
        remote(pack2_lo, got2_hi.at[:, W2 : W2 + nx], -1, 0),
        remote(pack2_hi.at[:, nx - W2 : nx], got2_lo.at[:, 0:W2], 1, 1),
        remote(pack2_hi.at[:, 0:W2], got2_lo.at[:, W2 + nx : 2 * W2 + nx], 1, -1),
        remote(pack2_lo.at[:, nx - W2 : nx], got2_hi.at[:, 0:W2], -1, 1),
        remote(pack2_lo.at[:, 0:W2], got2_hi.at[:, W2 + nx : 2 * W2 + nx], -1, -1),
        remote(field.at[0:3, W1 + nx - W2 : W1 + nx, 0:ny], side2_lo, 0, 1),
        remote(field.at[0:3, W1 : W1 + W2, 0:ny], side2_hi, 0, -1),
    ]

    total = mine[...]
    for d, copy in zip(range(1, n_col), part_copies):
        copy.wait_recv()
        total = total + partials[d]
    summed = lax.dot_general(
        jnp.ones((8, nz), jnp.float32),
        total,
        (((1,), (1,)), ((), ())),
        precision=lax.Precision.HIGHEST,
        preferred_element_type=jnp.float32,
    )
    grad_out[...] = summed[0:1] / math.sqrt(n_col * nx * ny * nz)

    for entry in second:
        arrived(entry)
    gap = jnp.zeros((8 - 2 * W2, nz), jnp.float32)

    def unpack2(x, _):
        for k in range(3):
            hi, lo = line_of(x, W2, got2_lo, got2_hi, k)
            field[k, x + W1 - W2, ny : ny + 8] = jnp.concatenate([hi, gap, lo], axis=0)
        return 0

    lax.fori_loop(0, nx + 2 * W2, unpack2, 0)
    for k in range(3):
        field[k, W1 - W2 : W1, 0:ny] = jnp.where(has[("col", -1)], side2_lo[k], 0.0)
        field[k, W1 + nx : W1 + nx + W2, 0:ny] = jnp.where(has[("col", 1)], side2_hi[k], 0.0)
    advance(field, other, W1 - 1, W1 + nx + 1, False)
    advance(other, mom_out, W1, W1 + nx, True)

    for entry in first[:-2] + level_sends + second:
        departed(entry)
    for copy in part_copies:
        copy.wait_send()


def local(
    n_row,
    n_col,
    level_cot,
    level_state,
    momentum_cot,
    courant,
    stencil,
    upwind,
    viscosity,
    band_cells,
    band_count,
    band_force,
    design_basis,
):
    nx, ny, nz = level_cot.shape
    ndes = design_basis.shape[0]
    basis = design_basis.reshape(ndes, nx * ny)
    wide, tall = nx + 2 * W1, ny + 8
    f32 = jnp.float32
    anywhere = pl.BlockSpec(memory_space=pl.ANY)
    vmem = pl.BlockSpec(memory_space=pltpu.VMEM)
    smem = pl.BlockSpec(memory_space=pltpu.SMEM)
    return pl.pallas_call(
        functools.partial(kernel, n_row, n_col),
        out_shape=(
            jax.ShapeDtypeStruct((nx, ny, nz), f32),
            jax.ShapeDtypeStruct((3, nx, ny, nz), f32),
            jax.ShapeDtypeStruct((1, ndes), f32),
        ),
        in_specs=[anywhere] * 7 + [vmem, smem, vmem, vmem],
        out_specs=(vmem, vmem, vmem),
        scratch_shapes=[
            pltpu.VMEM((4, wide, tall, nz), f32),
            pltpu.VMEM((3, wide, tall, nz), f32),
            pltpu.VMEM((7, wide, tall, nz), f32),
            pltpu.VMEM((3, nx + 2 * FACES, ny, nz), f32),
            pltpu.VMEM((2, nx + 2 * FACES, ny, nz), jnp.int32),
            pltpu.VMEM((nx * ny, 6 * nz), f32),
            pltpu.VMEM((nx * ny, nz), f32),
            pltpu.VMEM((4, nx, W1, nz), f32),
            pltpu.VMEM((4, nx, W1, nz), f32),
            pltpu.VMEM((4, wide, W1, nz), f32),
            pltpu.VMEM((4, wide, W1, nz), f32),
            pltpu.VMEM((3, nx, W2, nz), f32),
            pltpu.VMEM((3, nx, W2, nz), f32),
            pltpu.VMEM((3, nx + 2 * W2, W2, nz), f32),
            pltpu.VMEM((3, nx + 2 * W2, W2, nz), f32),
            pltpu.VMEM((3, W2, ny, nz), f32),
            pltpu.VMEM((3, W2, ny, nz), f32),
            pltpu.VMEM((ndes, nz), f32),
            pltpu.VMEM((n_col, ndes, nz), f32),
            pltpu.SemaphoreType.DMA((9,)),
            pltpu.SemaphoreType.DMA((20,)),
            pltpu.SemaphoreType.DMA((20,)),
            pltpu.SemaphoreType.DMA((n_col,)),
            pltpu.SemaphoreType.DMA((n_col,)),
        ],
        compiler_params=pltpu.CompilerParams(
            collective_id=0, has_side_effects=True, vmem_limit_bytes=50 * 1024 * 1024
        ),
    )(
        level_cot,
        level_state,
        momentum_cot,
        courant,
        stencil,
        upwind,
        viscosity,
        band_cells,
        band_count,
        band_force,
        basis,
    )


def solution(mesh):
    placed = (
        P("col", "row", None),
        P("col", "row", None),
        P(None, "col", "row", None),
        P("col", "row", None),
        P("col", "row", None),
        P("col", "row", None),
        P("col", "row", None),
        P("col", "row", None),
        P("col", "row"),
        P(None, "col", "row", None),
        P(None, "col", "row"),
    )
    return jax.shard_map(
        functools.partial(local, mesh.shape["row"], mesh.shape["col"]),
        mesh=mesh,
        in_specs=placed,
        out_specs=(P("col", "row", None), P(None, "col", "row", None), P("row", None)),
        check_vma=False,
    )
```

```python
import functools
import math

import jax
import jax.numpy as jnp
from jax import lax
from jax.experimental import pallas as pl
from jax.experimental.pallas import tpu as pltpu
from jax.sharding import PartitionSpec as P

MESH = pl.DeviceIdType.MESH
RATE = 0.05
W1 = 4
W2 = 2
CHUNK = 512
FACES = 3


def kernel(
    n_row,
    n_col,
    cot_hbm,
    state_hbm,
    mom_hbm,
    courant_hbm,
    stencil_hbm,
    upwind_hbm,
    visc_hbm,
    cells_hbm,
    count_ref,
    force_hbm,
    basis_hbm,
    level_out,
    mom_out,
    grad_out,
    field,
    other,
    coef,
    lev,
    codes,
    band_sum,
    product,
    pack_lo,
    pack_hi,
    got_lo,
    got_hi,
    pack2_lo,
    pack2_hi,
    got2_lo,
    got2_hi,
    side2_lo,
    side2_hi,
    mine,
    partials,
    cells_ref,
    force_ref,
    basis_ref,
    basis_flat,
    local_sem,
    send_sem,
    recv_sem,
    part_send,
    part_recv,
):
    nx, ny, nz = cot_hbm.shape
    row = lax.axis_index("row")
    col = lax.axis_index("col")
    has = {
        ("row", -1): row > 0,
        ("row", 1): row < n_row - 1,
        ("col", -1): col > 0,
        ("col", 1): col < n_col - 1,
    }

    def exists(dr, dc):
        cond = None
        for axis, d in (("row", dr), ("col", dc)):
            if d:
                here = has[(axis, d)]
                cond = here if cond is None else jnp.logical_and(cond, here)
        return cond

    barrier = pltpu.get_barrier_semaphore()
    expected = jnp.int32(n_col - 1)
    for d in range(1, n_col):
        pl.semaphore_signal(
            barrier, inc=1, device_id=(row, lax.rem(col + d, n_col)), device_id_type=MESH
        )
    for dr in (-1, 1):
        for dc in (-1, 0, 1):
            cond = exists(dr, dc)

            @pl.when(cond)
            def _(dr=dr, dc=dc):
                pl.semaphore_signal(
                    barrier, inc=1, device_id=(row + dr, col + dc), device_id_type=MESH
                )

            expected = expected + jnp.where(cond, 1, 0).astype(jnp.int32)

    local = []

    def fetch(src, dst):
        copy = pltpu.make_async_copy(src, dst, local_sem.at[len(local)])
        copy.start()
        local.append(copy)

    for k in range(3):
        fetch(mom_hbm.at[k], field.at[k, W1 : W1 + nx, 0:ny])
    fetch(visc_hbm, field.at[3, W1 : W1 + nx, 0:ny])
    for slot, src in enumerate((cot_hbm, state_hbm, courant_hbm)):
        fetch(src, lev.at[slot, FACES : FACES + nx])
    for slot, src in enumerate((stencil_hbm, upwind_hbm)):
        fetch(src, codes.at[slot, FACES : FACES + nx])
    fetch(cells_hbm, cells_ref)
    fetch(force_hbm, force_ref)
    fetch(basis_hbm, basis_ref)

    sends = []

    def remote(src, dst, dr, dc):
        i = len(sends)
        copy = pltpu.make_async_remote_copy(
            src_ref=src,
            dst_ref=dst,
            send_sem=send_sem.at[i],
            recv_sem=recv_sem.at[i],
            device_id=(row + dr, col + dc),
            device_id_type=MESH,
        )

        @pl.when(exists(dr, dc))
        def _():
            copy.start()

        sends.append((copy, dr, dc))
        return sends[-1]

    def arrived(entry):
        copy, dr, dc = entry

        @pl.when(exists(-dr, -dc))
        def _():
            copy.wait_recv()

    def departed(entry):
        copy, dr, dc = entry

        @pl.when(exists(dr, dc))
        def _():
            copy.wait_send()

    for copy in local[:4]:
        copy.wait()

    def pack(x, _):
        for k in range(4):
            pack_lo[k, x] = field[k, W1 + x, 0:8][0:W1]
            pack_hi[k, x] = field[k, W1 + x, ny - 8 : ny][8 - W1 : 8]
        return 0

    lax.fori_loop(0, nx, pack, 0, unroll=4)
    pl.semaphore_wait(barrier, expected)

    def line_sends(c):
        return [
            remote(pack_hi.at[c], got_lo.at[c, W1 : W1 + nx], 1, 0),
            remote(pack_lo.at[c], got_hi.at[c, W1 : W1 + nx], -1, 0),
            remote(pack_hi.at[c, nx - W1 : nx], got_lo.at[c, 0:W1], 1, 1),
            remote(pack_hi.at[c, 0:W1], got_lo.at[c, W1 + nx : 2 * W1 + nx], 1, -1),
            remote(pack_lo.at[c, nx - W1 : nx], got_hi.at[c, 0:W1], -1, 1),
            remote(pack_lo.at[c, 0:W1], got_hi.at[c, W1 + nx : 2 * W1 + nx], -1, -1),
        ]

    def plane_sends(c):
        return [
            remote(field.at[c, nx : nx + W1, 0:ny], field.at[c, 0:W1, 0:ny], 0, 1),
            remote(
                field.at[c, W1 : 2 * W1, 0:ny], field.at[c, nx + W1 : nx + 2 * W1, 0:ny], 0, -1
            ),
        ]

    mu_sends = line_sends(slice(3, 4))
    first = line_sends(slice(0, 3))
    for copy in local[4:]:
        copy.wait()
    level_sends = [
        remote(lev.at[:, nx : nx + FACES], lev.at[:, 0:FACES], 0, 1),
        remote(codes.at[:, nx : nx + FACES], codes.at[:, 0:FACES], 0, 1),
        remote(lev.at[:, FACES : 2 * FACES], lev.at[:, nx + FACES : nx + 2 * FACES], 0, -1),
        remote(codes.at[:, FACES : 2 * FACES], codes.at[:, nx + FACES : nx + 2 * FACES], 0, -1),
    ]
    mu_sends += plane_sends(slice(3, 4))
    first += plane_sends(slice(0, 3))

    count = count_ref[0, 0]
    band_cap = cells_ref.shape[-1]

    def band(step, _):
        at = pl.multiple_of(step * CHUNK, CHUNK)
        cell = cells_ref[0, :, pl.ds(at, CHUNK)]
        entry = at + lax.broadcasted_iota(jnp.int32, (1, CHUNK), 1)
        line = cell // nz
        z = cell - line * nz
        lines = lax.broadcasted_iota(jnp.int32, (nx * ny, CHUNK), 0) == line
        left = jnp.where(lines, 1.0, 0.0).astype(jnp.bfloat16)
        hit = lax.broadcasted_iota(jnp.int32, (nz, CHUNK), 0) == z
        parts = []
        for k in range(3):
            force = jnp.where(entry < count, force_ref[k, 0, :, pl.ds(at, CHUNK)], 0.0)
            high = force.astype(jnp.bfloat16).astype(jnp.float32)
            for part in (high, force - high):
                parts.append(jnp.where(hit, part, 0.0).astype(jnp.bfloat16))
        right = jnp.concatenate(parts, axis=0)
        total = lax.dot_general(
            left, right, (((1,), (1,)), ((), ())), preferred_element_type=jnp.float32
        )

        @pl.when(step == 0)
        def _():
            band_sum[...] = total

        @pl.when(step > 0)
        def _():
            band_sum[...] += total

        return 0

    lax.fori_loop(0, band_cap // CHUNK, band, 0)

    group = nz // ny
    for q in range(nx // group):
        basis_flat[:, q * nz : (q + 1) * nz] = jnp.concatenate(
            [basis_ref[:, q * group + i, :] for i in range(group)], axis=1
        )

    for entry in level_sends:
        arrived(entry)

    @pl.when(jnp.logical_not(has[("col", -1)]))
    def _():
        lev[:, 0:FACES] = jnp.zeros((3, FACES, ny, nz), jnp.float32)
        codes[:, 0:FACES] = jnp.zeros((2, FACES, ny, nz), jnp.int32)

    @pl.when(jnp.logical_not(has[("col", 1)]))
    def _():
        lev[:, nx + FACES : nx + 2 * FACES] = jnp.zeros((3, FACES, ny, nz), jnp.float32)
        codes[:, nx + FACES : nx + 2 * FACES] = jnp.zeros((2, FACES, ny, nz), jnp.int32)

    def face(e, carry, with_product, with_out):
        up = codes[1, e]
        sten = codes[0, e]
        below = up == 0
        is_a = jnp.logical_and(below, sten == 0)
        is_d = jnp.logical_and(jnp.logical_not(below), sten == 0)
        is_b = sten == jnp.where(below, 1, 2)
        g = col * nx + e - FACES
        inside = jnp.logical_and(g >= 0, g < n_col * nx - 1)
        speed = lev[2, e] * jnp.where(below, 1.0, -1.0)
        speed = jnp.where(inside, speed, 0.0)
        weighted = (lev[0, e + 1] - lev[0, e]) * speed
        zero = 0.0
        wts = (
            jnp.where(is_a, 1 / 3, zero),
            jnp.where(is_a, -7 / 6, jnp.where(is_b, -1 / 6, zero)),
            jnp.where(is_a, 11 / 6, jnp.where(is_b, 5 / 6, jnp.where(is_d, zero, 1 / 3))),
            jnp.where(is_d, 11 / 6, jnp.where(is_b, 1 / 3, jnp.where(is_a, zero, 5 / 6))),
            jnp.where(is_d, -7 / 6, jnp.where(jnp.logical_or(is_a, is_b), zero, -1 / 6)),
            jnp.where(is_d, 1 / 3, zero),
        )
        sums = [c + weighted * w for c, w in zip(carry, wts)]
        if with_product:
            value = wts[0] * lev[1, e - 2]
            for m in range(1, 6):
                value = value + wts[m] * lev[1, e - 2 + m]
            at = pl.multiple_of((e - FACES) * ny, ny)
            product[pl.ds(at, ny), :] = weighted * value
        if with_out:
            j = e - 5
            at = pl.multiple_of(j * ny, ny)
            strength = jnp.zeros((ny, nz), jnp.float32)
            for k in range(3):
                force = (
                    band_sum[pl.ds(at, ny), 2 * k * nz : (2 * k + 1) * nz]
                    + band_sum[pl.ds(at, ny), (2 * k + 1) * nz : (2 * k + 2) * nz]
                )
                strength = strength + force * field[k, W1 + j, 0:ny]
            bend = pltpu.roll(strength, 1, 1) + pltpu.roll(strength, nz - 1, 1) - 2.0 * strength
            level_out[j] = lev[0, j + FACES] + sums[0] + bend
        return tuple(sums[1:]) + (jnp.zeros((ny, nz), jnp.float32),)

    carry = tuple(jnp.zeros((ny, nz), jnp.float32) for _ in range(6))
    for low, high, with_product, with_out in (
        (0, 3, False, False),
        (3, 5, True, False),
        (5, nx + 3, True, True),
        (nx + 3, nx + 5, False, True),
    ):
        carry = lax.fori_loop(
            low,
            high,
            functools.partial(face, with_product=with_product, with_out=with_out),
            carry,
        )
    mine[...] = jnp.dot(
        basis_flat[...],
        product[...],
        precision=lax.Precision.HIGHEST,
        preferred_element_type=jnp.float32,
    )
    part_copies = []
    for d in range(1, n_col):
        copy = pltpu.make_async_remote_copy(
            src_ref=mine,
            dst_ref=partials.at[d],
            send_sem=part_send.at[d],
            recv_sem=part_recv.at[d],
            device_id=(row, lax.rem(col + d, n_col)),
            device_id_type=MESH,
        )
        copy.start()
        part_copies.append(copy)

    def line_of(x, width, lo_ref, hi_ref, k):
        left = x < width
        right = x >= width + nx
        in_col = jnp.logical_and(
            jnp.logical_or(jnp.logical_not(left), has[("col", -1)]),
            jnp.logical_or(jnp.logical_not(right), has[("col", 1)]),
        )
        hi = jnp.where(jnp.logical_and(in_col, has[("row", 1)]), hi_ref[k, x], 0.0)
        lo = jnp.where(jnp.logical_and(in_col, has[("row", -1)]), lo_ref[k, x], 0.0)
        return hi, lo

    def take(entries, low, high):
        for entry in entries:
            arrived(entry)

        def unpack(x, _):
            for k in range(low, high):
                hi, lo = line_of(x, W1, got_lo, got_hi, k)
                field[k, x, ny : ny + 8] = jnp.concatenate([hi, lo], axis=0)
            return 0

        lax.fori_loop(0, nx + 2 * W1, unpack, 0, unroll=4)
        blank = jnp.zeros((high - low, W1, ny, nz), jnp.float32)

        @pl.when(jnp.logical_not(has[("col", -1)]))
        def _():
            field[low:high, 0:W1, 0:ny] = blank

        @pl.when(jnp.logical_not(has[("col", 1)]))
        def _():
            field[low:high, nx + W1 : nx + 2 * W1, 0:ny] = blank

    take(mu_sends, 3, 4)
    tall = ny + 8
    sub = lax.broadcasted_iota(jnp.int32, (tall, nz), 0)
    lane = lax.broadcasted_iota(jnp.int32, (tall, nz), 1)
    up_there = jnp.where(has[("row", 1)], 1, 0)
    down_there = jnp.where(has[("row", -1)], 1, 0)
    y_inside = jnp.where(sub < ny, 1, jnp.where(sub < ny + 4, up_there, down_there)) > 0

    def coefficients(x, _):
        left = jnp.where(x < W1, jnp.where(has[("col", -1)], 1, 0), 1)
        right = jnp.where(x >= W1 + nx, jnp.where(has[("col", 1)], 1, 0), 1)
        inside = jnp.logical_and(y_inside, left * right > 0)
        mu = field[3, x]
        half = 0.5 * RATE
        near = [
            half * (mu + field[3, x + 1]),
            half * (mu + field[3, x - 1]),
            half * (mu + pltpu.roll(mu, tall - 1, 0)),
            half * (mu + pltpu.roll(mu, 1, 0)),
            half * (mu + jnp.where(lane == nz - 1, 0.0, pltpu.roll(mu, nz - 1, 1))),
            half * (mu + jnp.where(lane == 0, 0.0, pltpu.roll(mu, 1, 1))),
        ]
        own = 1.0 - (((near[0] + near[1]) + (near[2] + near[3])) + (near[4] + near[5]))
        near[4] = jnp.where(lane == nz - 1, 0.0, near[4])
        near[5] = jnp.where(lane == 0, 0.0, near[5])
        for slot, value in enumerate([own] + near):
            coef[slot, x] = jnp.where(inside, value, 0.0)
        return 0

    lax.fori_loop(1, nx + 2 * W1 - 1, coefficients, 0, unroll=2)
    take(first, 0, 3)

    def advance(src, dst, low, high, last):
        def one(x, _):
            for k in range(3):
                v = src[k, x]
                new = (
                    coef[0, x] * v
                    + coef[1, x] * src[k, x + 1]
                    + coef[2, x] * src[k, x - 1]
                    + coef[3, x] * pltpu.roll(v, tall - 1, 0)
                    + coef[4, x] * pltpu.roll(v, 1, 0)
                    + coef[5, x] * pltpu.roll(v, nz - 1, 1)
                    + coef[6, x] * pltpu.roll(v, 1, 1)
                )
                if last:
                    dst[k, x - W1] = new[0:ny]
                else:
                    dst[k, x] = new
            return 0

        lax.fori_loop(low, high, one, 0, unroll=2)

    end = nx + 2 * W1
    advance(field, other, 1, end - 1, False)
    for entry in first[-2:]:
        departed(entry)
    advance(other, field, 2, end - 2, False)
    advance(field, other, 3, end - 3, False)
    advance(other, field, 4, end - 4, False)

    def pack2(x, _):
        for k in range(3):
            pack2_lo[k, x] = field[k, W1 + x, 0:8][0:W2]
            pack2_hi[k, x] = field[k, W1 + x, ny - 8 : ny][8 - W2 : 8]
        return 0

    lax.fori_loop(0, nx, pack2, 0, unroll=4)
    second = [
        remote(pack2_hi, got2_lo.at[:, W2 : W2 + nx], 1, 0),
        remote(pack2_lo, got2_hi.at[:, W2 : W2 + nx], -1, 0),
        remote(pack2_hi.at[:, nx - W2 : nx], got2_lo.at[:, 0:W2], 1, 1),
        remote(pack2_hi.at[:, 0:W2], got2_lo.at[:, W2 + nx : 2 * W2 + nx], 1, -1),
        remote(pack2_lo.at[:, nx - W2 : nx], got2_hi.at[:, 0:W2], -1, 1),
        remote(pack2_lo.at[:, 0:W2], got2_hi.at[:, W2 + nx : 2 * W2 + nx], -1, -1),
        remote(field.at[0:3, W1 + nx - W2 : W1 + nx, 0:ny], side2_lo, 0, 1),
        remote(field.at[0:3, W1 : W1 + W2, 0:ny], side2_hi, 0, -1),
    ]

    total = mine[...]
    for d, copy in zip(range(1, n_col), part_copies):
        copy.wait_recv()
        total = total + partials[d]
    summed = lax.dot_general(
        jnp.ones((8, nz), jnp.float32),
        total,
        (((1,), (1,)), ((), ())),
        precision=lax.Precision.HIGHEST,
        preferred_element_type=jnp.float32,
    )
    grad_out[...] = summed[0:1] / math.sqrt(n_col * nx * ny * nz)

    for entry in second:
        arrived(entry)
    gap = jnp.zeros((8 - 2 * W2, nz), jnp.float32)

    def unpack2(x, _):
        for k in range(3):
            hi, lo = line_of(x, W2, got2_lo, got2_hi, k)
            field[k, x + W1 - W2, ny : ny + 8] = jnp.concatenate([hi, gap, lo], axis=0)
        return 0

    lax.fori_loop(0, nx + 2 * W2, unpack2, 0, unroll=4)
    for k in range(3):
        field[k, W1 - W2 : W1, 0:ny] = jnp.where(has[("col", -1)], side2_lo[k], 0.0)
        field[k, W1 + nx : W1 + nx + W2, 0:ny] = jnp.where(has[("col", 1)], side2_hi[k], 0.0)
    advance(field, other, W1 - 1, W1 + nx + 1, False)
    advance(other, mom_out, W1, W1 + nx, True)

    for entry in mu_sends + first[:-2] + level_sends + second:
        departed(entry)
    for copy in part_copies:
        copy.wait_send()


def local(
    n_row,
    n_col,
    level_cot,
    level_state,
    momentum_cot,
    courant,
    stencil,
    upwind,
    viscosity,
    band_cells,
    band_count,
    band_force,
    design_basis,
):
    nx, ny, nz = level_cot.shape
    ndes = design_basis.shape[0]
    wide, tall = nx + 2 * W1, ny + 8
    f32 = jnp.float32
    hbm = pl.BlockSpec(memory_space=pltpu.HBM)
    vmem = pl.BlockSpec(memory_space=pltpu.VMEM)
    smem = pl.BlockSpec(memory_space=pltpu.SMEM)
    return pl.pallas_call(
        functools.partial(kernel, n_row, n_col),
        out_shape=(
            jax.ShapeDtypeStruct((nx, ny, nz), f32),
            jax.ShapeDtypeStruct((3, nx, ny, nz), f32),
            jax.ShapeDtypeStruct((1, ndes), f32),
        ),
        in_specs=[hbm] * 8 + [smem, hbm, hbm],
        out_specs=(vmem, vmem, vmem),
        scratch_shapes=[
            pltpu.VMEM((4, wide, tall, nz), f32),
            pltpu.VMEM((3, wide, tall, nz), f32),
            pltpu.VMEM((7, wide, tall, nz), f32),
            pltpu.VMEM((3, nx + 2 * FACES, ny, nz), f32),
            pltpu.VMEM((2, nx + 2 * FACES, ny, nz), jnp.int32),
            pltpu.VMEM((nx * ny, 6 * nz), f32),
            pltpu.VMEM((nx * ny, nz), f32),
            pltpu.VMEM((4, nx, W1, nz), f32),
            pltpu.VMEM((4, nx, W1, nz), f32),
            pltpu.VMEM((4, wide, W1, nz), f32),
            pltpu.VMEM((4, wide, W1, nz), f32),
            pltpu.VMEM((3, nx, W2, nz), f32),
            pltpu.VMEM((3, nx, W2, nz), f32),
            pltpu.VMEM((3, nx + 2 * W2, W2, nz), f32),
            pltpu.VMEM((3, nx + 2 * W2, W2, nz), f32),
            pltpu.VMEM((3, W2, ny, nz), f32),
            pltpu.VMEM((3, W2, ny, nz), f32),
            pltpu.VMEM((ndes, nz), f32),
            pltpu.VMEM((n_col, ndes, nz), f32),
            pltpu.VMEM(band_cells.shape, jnp.int32),
            pltpu.VMEM(band_force.shape, f32),
            pltpu.VMEM(design_basis.shape, f32),
            pltpu.VMEM((ndes, nx * ny), f32),
            pltpu.SemaphoreType.DMA((12,)),
            pltpu.SemaphoreType.DMA((28,)),
            pltpu.SemaphoreType.DMA((28,)),
            pltpu.SemaphoreType.DMA((n_col,)),
            pltpu.SemaphoreType.DMA((n_col,)),
        ],
        compiler_params=pltpu.CompilerParams(
            collective_id=0, has_side_effects=True, vmem_limit_bytes=62 * 1024 * 1024
        ),
    )(
        level_cot,
        level_state,
        momentum_cot,
        courant,
        stencil,
        upwind,
        viscosity,
        band_cells,
        band_count,
        band_force,
        design_basis,
    )


def solution(mesh):
    placed = (
        P("col", "row", None),
        P("col", "row", None),
        P(None, "col", "row", None),
        P("col", "row", None),
        P("col", "row", None),
        P("col", "row", None),
        P("col", "row", None),
        P("col", "row", None),
        P("col", "row"),
        P(None, "col", "row", None),
        P(None, "col", "row"),
    )
    return jax.shard_map(
        functools.partial(local, mesh.shape["row"], mesh.shape["col"]),
        mesh=mesh,
        in_specs=placed,
        out_specs=(P("col", "row", None), P(None, "col", "row", None), P("row", None)),
        check_vma=False,
    )
```

```python
import functools
import math

import jax
import jax.numpy as jnp
from jax import lax
from jax.experimental import pallas as pl
from jax.experimental.pallas import tpu as pltpu
from jax.sharding import PartitionSpec as P

MESH = pl.DeviceIdType.MESH
RATE = 0.05
W1 = 4
W2 = 2
CHUNK = 512
FACES = 3
EARLY = 5


def kernel(
    n_row,
    n_col,
    cot_hbm,
    state_hbm,
    mom_hbm,
    courant_hbm,
    stencil_hbm,
    upwind_hbm,
    visc_hbm,
    cells_hbm,
    count_ref,
    force_hbm,
    basis_hbm,
    level_out,
    mom_out,
    grad_out,
    field,
    other,
    coef,
    lev,
    codes,
    band_sum,
    product,
    pack_lo,
    pack_hi,
    got_lo,
    got_hi,
    pack2_lo,
    pack2_hi,
    got2_lo,
    got2_hi,
    side2_lo,
    side2_hi,
    mine,
    partials,
    cells_ref,
    force_ref,
    basis_ref,
    basis_flat,
    cot_field,
    local_sem,
    send_sem,
    recv_sem,
    part_send,
    part_recv,
):
    nx, ny, nz = cot_hbm.shape
    row = lax.axis_index("row")
    col = lax.axis_index("col")
    has = {
        ("row", -1): row > 0,
        ("row", 1): row < n_row - 1,
        ("col", -1): col > 0,
        ("col", 1): col < n_col - 1,
    }

    def exists(dr, dc):
        cond = None
        for axis, d in (("row", dr), ("col", dc)):
            if d:
                here = has[(axis, d)]
                cond = here if cond is None else jnp.logical_and(cond, here)
        return cond

    barrier = pltpu.get_barrier_semaphore()
    expected = jnp.int32(n_col - 1)
    for d in range(1, n_col):
        pl.semaphore_signal(
            barrier, inc=1, device_id=(row, lax.rem(col + d, n_col)), device_id_type=MESH
        )
    for dr in (-1, 1):
        for dc in (-1, 0, 1):
            cond = exists(dr, dc)

            @pl.when(cond)
            def _(dr=dr, dc=dc):
                pl.semaphore_signal(
                    barrier, inc=1, device_id=(row + dr, col + dc), device_id_type=MESH
                )

            expected = expected + jnp.where(cond, 1, 0).astype(jnp.int32)

    local = []

    def fetch(src, dst):
        copy = pltpu.make_async_copy(src, dst, local_sem.at[len(local)])
        copy.start()
        local.append(copy)

    for k in range(3):
        fetch(mom_hbm.at[k], field.at[k, W1 : W1 + nx, 0:ny])
    fetch(visc_hbm, field.at[3, W1 : W1 + nx, 0:ny])
    for slot, src in enumerate((cot_hbm, state_hbm, courant_hbm)):
        fetch(src, lev.at[slot, FACES : FACES + nx])
    for slot, src in enumerate((stencil_hbm, upwind_hbm)):
        fetch(src, codes.at[slot, FACES : FACES + nx])
    fetch(cells_hbm, cells_ref)
    fetch(mom_hbm, cot_field)
    fetch(force_hbm, force_ref)
    fetch(basis_hbm, basis_ref)

    sends = []

    def remote(src, dst, dr, dc):
        i = len(sends)
        copy = pltpu.make_async_remote_copy(
            src_ref=src,
            dst_ref=dst,
            send_sem=send_sem.at[i],
            recv_sem=recv_sem.at[i],
            device_id=(row + dr, col + dc),
            device_id_type=MESH,
        )

        @pl.when(exists(dr, dc))
        def _():
            copy.start()

        sends.append((copy, dr, dc))
        return sends[-1]

    def arrived(entry):
        copy, dr, dc = entry

        @pl.when(exists(-dr, -dc))
        def _():
            copy.wait_recv()

    def departed(entry):
        copy, dr, dc = entry

        @pl.when(exists(dr, dc))
        def _():
            copy.wait_send()

    for copy in local[:4]:
        copy.wait()

    def pack(x, _):
        for k in range(4):
            pack_lo[k, x] = field[k, W1 + x, 0:8][0:W1]
            pack_hi[k, x] = field[k, W1 + x, ny - 8 : ny][8 - W1 : 8]
        return 0

    lax.fori_loop(0, nx, pack, 0, unroll=4)
    pl.semaphore_wait(barrier, expected)

    def line_sends(c):
        return [
            remote(pack_hi.at[c], got_lo.at[c, W1 : W1 + nx], 1, 0),
            remote(pack_lo.at[c], got_hi.at[c, W1 : W1 + nx], -1, 0),
            remote(pack_hi.at[c, nx - W1 : nx], got_lo.at[c, 0:W1], 1, 1),
            remote(pack_hi.at[c, 0:W1], got_lo.at[c, W1 + nx : 2 * W1 + nx], 1, -1),
            remote(pack_lo.at[c, nx - W1 : nx], got_hi.at[c, 0:W1], -1, 1),
            remote(pack_lo.at[c, 0:W1], got_hi.at[c, W1 + nx : 2 * W1 + nx], -1, -1),
        ]

    def plane_sends(c):
        return [
            remote(field.at[c, nx : nx + W1, 0:ny], field.at[c, 0:W1, 0:ny], 0, 1),
            remote(
                field.at[c, W1 : 2 * W1, 0:ny], field.at[c, nx + W1 : nx + 2 * W1, 0:ny], 0, -1
            ),
        ]

    mu_sends = line_sends(slice(3, 4))
    first = line_sends(slice(0, 3))
    for copy in local[4:]:
        copy.wait()
    level_sends = [
        remote(lev.at[:, nx : nx + FACES], lev.at[:, 0:FACES], 0, 1),
        remote(codes.at[:, nx : nx + FACES], codes.at[:, 0:FACES], 0, 1),
        remote(lev.at[:, FACES : 2 * FACES], lev.at[:, nx + FACES : nx + 2 * FACES], 0, -1),
        remote(codes.at[:, FACES : 2 * FACES], codes.at[:, nx + FACES : nx + 2 * FACES], 0, -1),
    ]
    mu_sends += plane_sends(slice(3, 4))
    first += plane_sends(slice(0, 3))

    count = count_ref[0, 0]
    band_cap = cells_ref.shape[-1]

    def band(step, _):
        at = pl.multiple_of(step * CHUNK, CHUNK)
        cell = cells_ref[0, :, pl.ds(at, CHUNK)]
        entry = at + lax.broadcasted_iota(jnp.int32, (1, CHUNK), 1)
        line = cell // nz
        z = cell - line * nz
        lines = lax.broadcasted_iota(jnp.int32, (nx * ny, CHUNK), 0) == line
        left = jnp.where(lines, 1.0, 0.0).astype(jnp.bfloat16)
        hit = lax.broadcasted_iota(jnp.int32, (nz, CHUNK), 0) == z
        parts = []
        for k in range(3):
            force = jnp.where(entry < count, force_ref[k, 0, :, pl.ds(at, CHUNK)], 0.0)
            high = force.astype(jnp.bfloat16).astype(jnp.float32)
            for part in (high, force - high):
                parts.append(jnp.where(hit, part, 0.0).astype(jnp.bfloat16))
        right = jnp.concatenate(parts, axis=0)
        total = lax.dot_general(
            left, right, (((1,), (1,)), ((), ())), preferred_element_type=jnp.float32
        )

        @pl.when(step == 0)
        def _():
            band_sum[...] = total

        @pl.when(step > 0)
        def _():
            band_sum[...] += total

        return 0

    chunks = band_cap // CHUNK
    early = chunks * EARLY // 8
    lax.fori_loop(0, early, band, 0)

    group = nz // ny
    for q in range(nx // group):
        basis_flat[:, q * nz : (q + 1) * nz] = jnp.concatenate(
            [basis_ref[:, q * group + i, :] for i in range(group)], axis=1
        )

    for entry in level_sends:
        arrived(entry)

    @pl.when(jnp.logical_not(has[("col", -1)]))
    def _():
        lev[:, 0:FACES] = jnp.zeros((3, FACES, ny, nz), jnp.float32)
        codes[:, 0:FACES] = jnp.zeros((2, FACES, ny, nz), jnp.int32)

    @pl.when(jnp.logical_not(has[("col", 1)]))
    def _():
        lev[:, nx + FACES : nx + 2 * FACES] = jnp.zeros((3, FACES, ny, nz), jnp.float32)
        codes[:, nx + FACES : nx + 2 * FACES] = jnp.zeros((2, FACES, ny, nz), jnp.int32)

    def face(e, carry, with_product, with_out):
        up = codes[1, e]
        sten = codes[0, e]
        below = up == 0
        is_a = jnp.logical_and(below, sten == 0)
        is_d = jnp.logical_and(jnp.logical_not(below), sten == 0)
        is_b = sten == jnp.where(below, 1, 2)
        g = col * nx + e - FACES
        inside = jnp.logical_and(g >= 0, g < n_col * nx - 1)
        speed = lev[2, e] * jnp.where(below, 1.0, -1.0)
        speed = jnp.where(inside, speed, 0.0)
        weighted = (lev[0, e + 1] - lev[0, e]) * speed
        zero = 0.0
        wts = (
            jnp.where(is_a, 1 / 3, zero),
            jnp.where(is_a, -7 / 6, jnp.where(is_b, -1 / 6, zero)),
            jnp.where(is_a, 11 / 6, jnp.where(is_b, 5 / 6, jnp.where(is_d, zero, 1 / 3))),
            jnp.where(is_d, 11 / 6, jnp.where(is_b, 1 / 3, jnp.where(is_a, zero, 5 / 6))),
            jnp.where(is_d, -7 / 6, jnp.where(jnp.logical_or(is_a, is_b), zero, -1 / 6)),
            jnp.where(is_d, 1 / 3, zero),
        )
        sums = [c + weighted * w for c, w in zip(carry, wts)]
        if with_product:
            value = wts[0] * lev[1, e - 2]
            for m in range(1, 6):
                value = value + wts[m] * lev[1, e - 2 + m]
            at = pl.multiple_of((e - FACES) * ny, ny)
            product[pl.ds(at, ny), :] = weighted * value
        if with_out:
            j = e - 5
            level_out[j] = lev[0, j + FACES] + sums[0]
        return tuple(sums[1:]) + (jnp.zeros((ny, nz), jnp.float32),)

    carry = tuple(jnp.zeros((ny, nz), jnp.float32) for _ in range(6))
    for low, high, with_product, with_out in (
        (0, 3, False, False),
        (3, 5, True, False),
        (5, nx + 3, True, True),
        (nx + 3, nx + 5, False, True),
    ):
        carry = lax.fori_loop(
            low,
            high,
            functools.partial(face, with_product=with_product, with_out=with_out),
            carry,
        )
    mine[...] = jnp.dot(
        basis_flat[...],
        product[...],
        precision=lax.Precision.HIGHEST,
        preferred_element_type=jnp.float32,
    )
    part_copies = []
    for d in range(1, n_col):
        copy = pltpu.make_async_remote_copy(
            src_ref=mine,
            dst_ref=partials.at[d],
            send_sem=part_send.at[d],
            recv_sem=part_recv.at[d],
            device_id=(row, lax.rem(col + d, n_col)),
            device_id_type=MESH,
        )
        copy.start()
        part_copies.append(copy)

    def line_of(x, width, lo_ref, hi_ref, k):
        left = x < width
        right = x >= width + nx
        in_col = jnp.logical_and(
            jnp.logical_or(jnp.logical_not(left), has[("col", -1)]),
            jnp.logical_or(jnp.logical_not(right), has[("col", 1)]),
        )
        hi = jnp.where(jnp.logical_and(in_col, has[("row", 1)]), hi_ref[k, x], 0.0)
        lo = jnp.where(jnp.logical_and(in_col, has[("row", -1)]), lo_ref[k, x], 0.0)
        return hi, lo

    def take(entries, low, high):
        for entry in entries:
            arrived(entry)

        def unpack(x, _):
            for k in range(low, high):
                hi, lo = line_of(x, W1, got_lo, got_hi, k)
                field[k, x, ny : ny + 8] = jnp.concatenate([hi, lo], axis=0)
            return 0

        lax.fori_loop(0, nx + 2 * W1, unpack, 0, unroll=4)
        blank = jnp.zeros((high - low, W1, ny, nz), jnp.float32)

        @pl.when(jnp.logical_not(has[("col", -1)]))
        def _():
            field[low:high, 0:W1, 0:ny] = blank

        @pl.when(jnp.logical_not(has[("col", 1)]))
        def _():
            field[low:high, nx + W1 : nx + 2 * W1, 0:ny] = blank

    take(mu_sends, 3, 4)
    tall = ny + 8
    sub = lax.broadcasted_iota(jnp.int32, (tall, nz), 0)
    lane = lax.broadcasted_iota(jnp.int32, (tall, nz), 1)
    up_there = jnp.where(has[("row", 1)], 1, 0)
    down_there = jnp.where(has[("row", -1)], 1, 0)
    y_inside = jnp.where(sub < ny, 1, jnp.where(sub < ny + 4, up_there, down_there)) > 0

    def coefficients(x, _):
        left = jnp.where(x < W1, jnp.where(has[("col", -1)], 1, 0), 1)
        right = jnp.where(x >= W1 + nx, jnp.where(has[("col", 1)], 1, 0), 1)
        inside = jnp.logical_and(y_inside, left * right > 0)
        mu = field[3, x]
        half = 0.5 * RATE
        near = [
            half * (mu + field[3, x + 1]),
            half * (mu + field[3, x - 1]),
            half * (mu + pltpu.roll(mu, tall - 1, 0)),
            half * (mu + pltpu.roll(mu, 1, 0)),
            half * (mu + jnp.where(lane == nz - 1, 0.0, pltpu.roll(mu, nz - 1, 1))),
            half * (mu + jnp.where(lane == 0, 0.0, pltpu.roll(mu, 1, 1))),
        ]
        own = 1.0 - (((near[0] + near[1]) + (near[2] + near[3])) + (near[4] + near[5]))
        near[4] = jnp.where(lane == nz - 1, 0.0, near[4])
        near[5] = jnp.where(lane == 0, 0.0, near[5])
        for slot, value in enumerate([own] + near):
            coef[slot, x] = jnp.where(inside, value, 0.0)
        return 0

    lax.fori_loop(1, nx + 2 * W1 - 1, coefficients, 0, unroll=2)
    take(first, 0, 3)

    def advance(src, dst, low, high, last):
        def one(x, _):
            for k in range(3):
                v = src[k, x]
                new = (
                    coef[0, x] * v
                    + coef[1, x] * src[k, x + 1]
                    + coef[2, x] * src[k, x - 1]
                    + coef[3, x] * pltpu.roll(v, tall - 1, 0)
                    + coef[4, x] * pltpu.roll(v, 1, 0)
                    + coef[5, x] * pltpu.roll(v, nz - 1, 1)
                    + coef[6, x] * pltpu.roll(v, 1, 1)
                )
                if last:
                    dst[k, x - W1] = new[0:ny]
                else:
                    dst[k, x] = new
            return 0

        lax.fori_loop(low, high, one, 0, unroll=4 if (high - low) % 4 == 0 else 2)

    end = nx + 2 * W1
    advance(field, other, 1, end - 1, False)
    for entry in first[-2:]:
        departed(entry)
    advance(other, field, 2, end - 2, False)
    advance(field, other, 3, end - 3, False)
    advance(other, field, 4, end - 4, False)

    def pack2(x, _):
        for k in range(3):
            pack2_lo[k, x] = field[k, W1 + x, 0:8][0:W2]
            pack2_hi[k, x] = field[k, W1 + x, ny - 8 : ny][8 - W2 : 8]
        return 0

    lax.fori_loop(0, nx, pack2, 0, unroll=4)
    second = [
        remote(pack2_hi, got2_lo.at[:, W2 : W2 + nx], 1, 0),
        remote(pack2_lo, got2_hi.at[:, W2 : W2 + nx], -1, 0),
        remote(pack2_hi.at[:, nx - W2 : nx], got2_lo.at[:, 0:W2], 1, 1),
        remote(pack2_hi.at[:, 0:W2], got2_lo.at[:, W2 + nx : 2 * W2 + nx], 1, -1),
        remote(pack2_lo.at[:, nx - W2 : nx], got2_hi.at[:, 0:W2], -1, 1),
        remote(pack2_lo.at[:, 0:W2], got2_hi.at[:, W2 + nx : 2 * W2 + nx], -1, -1),
        remote(field.at[0:3, W1 + nx - W2 : W1 + nx, 0:ny], side2_lo, 0, 1),
        remote(field.at[0:3, W1 : W1 + W2, 0:ny], side2_hi, 0, -1),
    ]

    total = mine[...]
    for d, copy in zip(range(1, n_col), part_copies):
        copy.wait_recv()
        total = total + partials[d]
    summed = lax.dot_general(
        jnp.ones((8, nz), jnp.float32),
        total,
        (((1,), (1,)), ((), ())),
        precision=lax.Precision.HIGHEST,
        preferred_element_type=jnp.float32,
    )
    grad_out[...] = summed[0:1] / math.sqrt(n_col * nx * ny * nz)

    lax.fori_loop(early, chunks, band, 0)

    def tension(j, _):
        at = pl.multiple_of(j * ny, ny)
        strength = jnp.zeros((ny, nz), jnp.float32)
        for k in range(3):
            force = (
                band_sum[pl.ds(at, ny), 2 * k * nz : (2 * k + 1) * nz]
                + band_sum[pl.ds(at, ny), (2 * k + 1) * nz : (2 * k + 2) * nz]
            )
            strength = strength + force * cot_field[k, j]
        bend = pltpu.roll(strength, 1, 1) + pltpu.roll(strength, nz - 1, 1) - 2.0 * strength
        level_out[j] += bend
        return 0

    lax.fori_loop(0, nx, tension, 0, unroll=4)

    for entry in second:
        arrived(entry)
    gap = jnp.zeros((8 - 2 * W2, nz), jnp.float32)

    def unpack2(x, _):
        for k in range(3):
            hi, lo = line_of(x, W2, got2_lo, got2_hi, k)
            field[k, x + W1 - W2, ny : ny + 8] = jnp.concatenate([hi, gap, lo], axis=0)
        return 0

    lax.fori_loop(0, nx + 2 * W2, unpack2, 0, unroll=4)
    for k in range(3):
        field[k, W1 - W2 : W1, 0:ny] = jnp.where(has[("col", -1)], side2_lo[k], 0.0)
        field[k, W1 + nx : W1 + nx + W2, 0:ny] = jnp.where(has[("col", 1)], side2_hi[k], 0.0)
    advance(field, other, W1 - 1, W1 + nx + 1, False)
    advance(other, mom_out, W1, W1 + nx, True)

    for entry in mu_sends + first[:-2] + level_sends + second:
        departed(entry)
    for copy in part_copies:
        copy.wait_send()


def deliver(level_in, mom_in, grad_in, level_out, mom_out, grad_out, level, mom, grad, sem):
    trips = [(grad_in, grad, grad_out)]
    for src, mid, dst in [(level_in, level, level_out)] + [
        (mom_in.at[k], mom.at[k], mom_out.at[k]) for k in range(3)
    ]:
        half = src.shape[0] // 2
        for at in (0, half):
            part = slice(at, at + half)
            trips.append((src.at[part], mid.at[part], dst.at[part]))
    loads = [pltpu.make_async_copy(a, b, sem.at[0, i]) for i, (a, b, _) in enumerate(trips)]
    stores = [pltpu.make_async_copy(b, c, sem.at[1, i]) for i, (_, b, c) in enumerate(trips)]
    for copy in loads:
        copy.start()
    for load, store in zip(loads, stores):
        load.wait()
        store.start()
    for copy in stores:
        copy.wait()


def local(
    n_row,
    n_col,
    level_cot,
    level_state,
    momentum_cot,
    courant,
    stencil,
    upwind,
    viscosity,
    band_cells,
    band_count,
    band_force,
    design_basis,
):
    nx, ny, nz = level_cot.shape
    ndes = design_basis.shape[0]
    wide, tall = nx + 2 * W1, ny + 8
    f32 = jnp.float32
    hbm = pl.BlockSpec(memory_space=pltpu.HBM)
    vmem = pl.BlockSpec(memory_space=pltpu.VMEM)
    smem = pl.BlockSpec(memory_space=pltpu.SMEM)
    made = pl.pallas_call(
        functools.partial(kernel, n_row, n_col),
        out_shape=(
            jax.ShapeDtypeStruct((nx, ny, nz), f32),
            jax.ShapeDtypeStruct((3, nx, ny, nz), f32),
            jax.ShapeDtypeStruct((1, ndes), f32),
        ),
        in_specs=[hbm] * 8 + [smem, hbm, hbm],
        out_specs=(vmem, vmem, vmem),
        scratch_shapes=[
            pltpu.VMEM((4, wide, tall, nz), f32),
            pltpu.VMEM((3, wide, tall, nz), f32),
            pltpu.VMEM((7, wide, tall, nz), f32),
            pltpu.VMEM((3, nx + 2 * FACES, ny, nz), f32),
            pltpu.VMEM((2, nx + 2 * FACES, ny, nz), jnp.int32),
            pltpu.VMEM((nx * ny, 6 * nz), f32),
            pltpu.VMEM((nx * ny, nz), f32),
            pltpu.VMEM((4, nx, W1, nz), f32),
            pltpu.VMEM((4, nx, W1, nz), f32),
            pltpu.VMEM((4, wide, W1, nz), f32),
            pltpu.VMEM((4, wide, W1, nz), f32),
            pltpu.VMEM((3, nx, W2, nz), f32),
            pltpu.VMEM((3, nx, W2, nz), f32),
            pltpu.VMEM((3, nx + 2 * W2, W2, nz), f32),
            pltpu.VMEM((3, nx + 2 * W2, W2, nz), f32),
            pltpu.VMEM((3, W2, ny, nz), f32),
            pltpu.VMEM((3, W2, ny, nz), f32),
            pltpu.VMEM((ndes, nz), f32),
            pltpu.VMEM((n_col, ndes, nz), f32),
            pltpu.VMEM(band_cells.shape, jnp.int32),
            pltpu.VMEM(band_force.shape, f32),
            pltpu.VMEM(design_basis.shape, f32),
            pltpu.VMEM((ndes, nx * ny), f32),
            pltpu.VMEM((3, nx, ny, nz), f32),
            pltpu.SemaphoreType.DMA((13,)),
            pltpu.SemaphoreType.DMA((28,)),
            pltpu.SemaphoreType.DMA((28,)),
            pltpu.SemaphoreType.DMA((n_col,)),
            pltpu.SemaphoreType.DMA((n_col,)),
        ],
        compiler_params=pltpu.CompilerParams(
            collective_id=0, has_side_effects=True, vmem_limit_bytes=62 * 1024 * 1024
        ),
    )(
        level_cot,
        level_state,
        momentum_cot,
        courant,
        stencil,
        upwind,
        viscosity,
        band_cells,
        band_count,
        band_force,
        design_basis,
    )
    return pl.pallas_call(
        deliver,
        out_shape=tuple(jax.ShapeDtypeStruct(x.shape, x.dtype) for x in made),
        in_specs=[hbm] * 3,
        out_specs=(hbm,) * 3,
        scratch_shapes=[pltpu.VMEM(x.shape, x.dtype) for x in made]
        + [pltpu.SemaphoreType.DMA((2, 9))],
        compiler_params=pltpu.CompilerParams(vmem_limit_bytes=62 * 1024 * 1024),
    )(*made)


def solution(mesh):
    placed = (
        P("col", "row", None),
        P("col", "row", None),
        P(None, "col", "row", None),
        P("col", "row", None),
        P("col", "row", None),
        P("col", "row", None),
        P("col", "row", None),
        P("col", "row", None),
        P("col", "row"),
        P(None, "col", "row", None),
        P(None, "col", "row"),
    )
    return jax.shard_map(
        functools.partial(local, mesh.shape["row"], mesh.shape["col"]),
        mesh=mesh,
        in_specs=placed,
        out_specs=(P("col", "row", None), P(None, "col", "row", None), P("row", None)),
        check_vma=False,
    )
```
